32 devices in a mesh: fsdp: 16 (over z, y, core), rep: 2 (over x).
Axes of the slice: x: 2, y: 2, z: 4, core: 2. Of those that a mesh axis runs over, the one named last changes fastest.
Arguments:
- tokens: bfloat16 [32768, 1024], P(('fsdp', 'rep')), may hold values from -6 to 6
- segment_ids: int32 [32768], P(('fsdp', 'rep')), may hold values from 0 to 47, as said below
- in_weight: bfloat16 [1024, 4384], P(('fsdp', 'rep')), may hold values from -0.1875 to 0.1875
- out_weight: bfloat16 [2048, 1024], P(None, ('fsdp', 'rep')), may hold values from -0.125 to 0.125
- conv_weight: bfloat16 [4, 2304], P(None, ('fsdp', 'rep')), may hold values from -4 to 4
- conv_bias: bfloat16 [2304], P(('fsdp', 'rep')), may hold values from -3 to 3
- norm_gain: bfloat16 [1024], P(('fsdp', 'rep')), may hold values from 0.5 to 1.5
- gate_gain: bfloat16 [2048], P(('fsdp', 'rep')), may hold values from 0.5 to 1.5
- step_bias: float32 [32], replicated, may hold values from -4 to -2
- decay_log: float32 [32], replicated, may hold values from -4 to 0
- skip_gain: float32 [32], replicated, may hold values from 0.5 to 2
- cotangent: bfloat16 [32768, 1024], P(('fsdp', 'rep')), may hold values from -6 to 6
Outputs:
- mixed: bfloat16 [32768, 1024], P(('fsdp', 'rep'))
- grad_tokens: bfloat16 [32768, 1024], P(('fsdp', 'rep'))
- grad_in_weight: float32 [1024, 4384], P(('fsdp', 'rep'))
- grad_out_weight: float32 [2048, 1024], P(None, ('fsdp', 'rep'))
- grad_conv_weight: float32 [4, 2304], P(None, ('fsdp', 'rep'))
- grad_conv_bias: float32 [2304], P(('fsdp', 'rep'))
- grad_norm_gain: float32 [1024], P(('fsdp', 'rep'))
- grad_gate_gain: float32 [2048], P(('fsdp', 'rep'))
- grad_step_bias: float32 [32], replicated
- grad_decay_log: float32 [32], replicated
- grad_skip_gain: float32 [32], replicated
The draws below stay inside these ranges and needn't reach their ends.
Inputs may be any that keep to these rules, and one draw needn't show every extreme that they name: `segment_ids`: segment ids never fall and are numbered 0, 1, 2, ... in order; every device's block of 1024 tokens begins a new segment and no segment crosses the end of such a block; the first block is one whole segment; of the other blocks exactly (32768 // 1024) // 2 hold two segments, the second beginning at a multiple of 64 no earlier than 256 and no later than 768 tokens into the block, and the rest hold one.
All inputs are finite; a program needn't handle non-finite values.
Results may differ from the reference program's by a relative error of at most 0.0057.
Values may be sent and summed in bfloat16 or wider, within the bound.
A program may use at most 256 MiB of HBM per device.

```python
import jax
import jax.numpy as jnp
from jax import lax

D = 1024
HEADS = 32
CONV = 4
SPAN = 256
TOK_DEV = 1024
INNER = 2048
XBC = 2304
PROJ = 4384
TOKENS = 32768


def draw_segment_ids(key, part):
    key = jax.random.fold_in(key, 11)
    stride = SPAN // 4
    block_count = TOKENS // TOK_DEV
    split_lo = TOK_DEV // 4 // stride
    split_hi = 3 * TOK_DEV // 4 // stride
    pick_key = jax.random.fold_in(key, 1)
    place_key = jax.random.fold_in(key, 2)
    order = jax.random.permutation(pick_key, block_count - 1)
    doubled = jnp.concatenate([jnp.zeros((1,), jnp.int32), (order < block_count // 2).astype(jnp.int32)])
    split_at = jax.random.randint(place_key, (block_count,), split_lo, split_hi + 1).astype(jnp.int32) * stride
    positions = jnp.arange(TOK_DEV, dtype=jnp.int32)
    first_flag = (positions == 0).astype(jnp.int32)[None, :]
    second_flag = (positions[None, :] == split_at[:, None]).astype(jnp.int32) * doubled[:, None]
    start_flags = (first_flag + second_flag).reshape(TOKENS)
    return (jnp.cumsum(start_flags) - 1).astype(jnp.int32)


def spiked(values, stream_key, source, target, shards_of, factor):
    def block_of(axis_at):
        return (jnp.arange(values.shape[axis_at]) // (values.shape[axis_at] // shards_of)).reshape((-1,) + (1,) * (values.ndim - 1 - axis_at))

    near = jax.random.permutation(stream_key, shards_of)[block_of(target)]
    other_side = (block_of(target) + shards_of // 2) % shards_of
    return jnp.where((block_of(source) == near) | (block_of(source) == other_side), factor * values, values)


def levels(rng, extent, cuts, low, high):
    level = 1.0
    for dim, shards_of in cuts:
        draws = jax.random.uniform(jax.random.fold_in(jax.random.fold_in(rng, 6), dim), (shards_of,), jnp.float32, low / len(cuts), high / len(cuts))
        level = level * jnp.repeat(jnp.exp(draws), extent[dim] // shards_of).reshape((-1,) + (1,) * (len(extent) - 1 - dim))
    return level


def noise(own_key, extent, deviation, reach, shards=(), held_as=jnp.bfloat16):
    values = jax.random.normal(own_key, extent, jnp.float32) * deviation
    if len(shards) > 0:
        values = levels(own_key, extent, shards, -0.22, 0.18) * values
    return jnp.clip(values, min=-reach, max=reach).astype(held_as)


def gaussian_with(rng, dims, deviation, bound, split, heavy, kind=jnp.bfloat16):
    entries = deviation * jax.random.normal(rng, dims, jnp.float32)
    if split:
        entries = entries * levels(rng, dims, split, -0.22, 0.18)
    return jnp.clip(spiked(entries, jax.random.fold_in(rng, 3), *heavy), -bound, bound).astype(kind)


def setup_inputs(seed: int = 0) -> dict:
    keys = jax.random.split(jax.random.key(seed), 13)
    tokens = gaussian_with(keys[0], (TOKENS, D), 1.0, 6.0, ((0, 32),), (0, 1, 32, 2.75))
    segment_ids = draw_segment_ids(jax.random.fold_in(keys[12], 71), 0)
    in_weight = noise(keys[2], (D, PROJ), D ** -0.5, 0.1875, ((0, 32),))
    out_weight = noise(keys[3], (INNER, D), INNER ** -0.5, 0.125, ((1, 32),))
    conv_weight = noise(keys[4], (CONV, XBC), 2 ** -0.5, 4.0, ((1, 32),))
    conv_bias = noise(keys[5], (XBC,), 0.5, 3.0, ((0, 32),))
    norm_gain = jnp.clip(1.0 + 0.1 * jax.random.normal(keys[6], (D,), jnp.float32), 0.5, 1.5).astype(jnp.bfloat16)
    gate_gain = jnp.clip(1.0 + 0.1 * jax.random.normal(keys[7], (INNER,), jnp.float32), 0.5, 1.5).astype(jnp.bfloat16)
    step_bias = jnp.clip(jax.random.uniform(keys[8], (HEADS,), jnp.float32, -4.0, -2.0), -4.0, -2.0)
    decay_log = jnp.clip(jax.random.uniform(keys[9], (HEADS,), jnp.float32, -4.0, 0.0), -4.0, 0.0)
    skip_gain = jnp.clip(jax.random.uniform(keys[10], (HEADS,), jnp.float32, 0.5, 2.0), 0.5, 2.0)
    cotangent = gaussian_with(keys[11], (TOKENS, D), 1.0, 6.0, ((0, 32),), (0, 1, 32, 2.75))
    return {"tokens": tokens, "segment_ids": segment_ids, "in_weight": in_weight, "out_weight": out_weight, "conv_weight": conv_weight, "conv_bias": conv_bias, "norm_gain": norm_gain, "gate_gain": gate_gain, "step_bias": step_bias, "decay_log": decay_log, "skip_gain": skip_gain, "cotangent": cotangent}


@jax.custom_vjp
def low(v):
    return lax.optimization_barrier(v.astype(jnp.bfloat16)).astype(jnp.float32)

@jax.custom_vjp
def low_back(v):
    return v

def low_keep(v):
    return (low(v), None)

def low_pass(kept, grad):
    return (grad,)

def back_keep(v):
    return (v, None)

def back_low(kept, grad):
    return (low(grad),)
low.defvjp(low_keep, low_pass)
low_back.defvjp(back_keep, back_low)
epsilon = 1e-05

def span_scan(head_flat, step_size, log_rate, input_map, output_map, seg_rows, span_len, head_count):
    tok_count, inner_size = head_flat.shape
    head_size = inner_size // head_count
    state_size = input_map.shape[1]
    block_count = tok_count // span_len
    highest = lax.Precision.HIGHEST

    def to_spans(values):
        return values.reshape((block_count, span_len) + values.shape[1:])

    def span_step(carried, pieces):
        state_held, prior_seg = carried
        flat_part, size_part, rate_part, in_part, out_part, seg_part = pieces
        x_part = flat_part.reshape(span_len, head_count, head_size)
        cumul = jnp.cumsum(rate_part, axis=0)
        cumul_t = cumul.T
        log_gap = cumul_t[:, :, None] - cumul_t[:, None, :]
        rows_idx = lax.broadcasted_iota(jnp.int32, (span_len, span_len), 0)
        cols_idx = lax.broadcasted_iota(jnp.int32, (span_len, span_len), 1)
        same_seg = (seg_part[:, None] == seg_part[None, :]) & (rows_idx >= cols_idx)
        decay_mask = jnp.where(same_seg[None, :, :], jnp.exp(jnp.minimum(log_gap, 0.0)), 0.0)
        scores = jnp.dot(out_part, in_part.T, precision=highest)
        scaled_x = x_part * size_part[:, :, None]
        inside = jnp.einsum('hts,ts,shp->thp', decay_mask, scores, scaled_x, precision=highest)
        entering = (seg_part == prior_seg).astype(x_part.dtype)
        carried_in = jnp.einsum('tn,hpn->thp', out_part, state_held, precision=highest)
        carried_in = carried_in * (jnp.exp(cumul) * entering[:, None])[:, :, None]
        final_seg = seg_part[span_len - 1]
        tail_decay = jnp.exp(cumul[span_len - 1][None, :] - cumul) * (seg_part == final_seg).astype(x_part.dtype)[:, None]
        keep_rate = jnp.exp(cumul[span_len - 1]) * (final_seg == prior_seg).astype(x_part.dtype)
        state_held = keep_rate[:, None, None] * state_held + jnp.einsum('sh,sn,shp->hpn', tail_decay, in_part, scaled_x, precision=highest)
        return ((state_held, final_seg), (inside + carried_in).reshape(span_len, inner_size))
    start_state = (jnp.zeros((head_count, head_size, state_size), head_flat.dtype), jnp.array(-1, jnp.int32))
    pieces = tuple((to_spans(values) for values in (head_flat, step_size, log_rate, input_map, output_map, seg_rows)))
    unused, outputs = lax.scan(jax.checkpoint(span_step), start_state, pieces)
    return outputs.reshape(tok_count, inner_size)

def mixer(proj, conv_weight, conv_bias, step_bias, decay_log, skip_gain, gate_gain, seg_rows, span_len):
    inner_size = gate_gain.shape[0]
    head_count = step_bias.shape[0]
    width_xbc = conv_weight.shape[1]
    conv_size = conv_weight.shape[0]
    state_size = (width_xbc - inner_size) // 2
    head_size = inner_size // head_count
    tok_count = proj.shape[0]
    gate_in = proj[:, :inner_size]
    conv_in = proj[:, inner_size:inner_size + width_xbc]
    step_raw = proj[:, inner_size + width_xbc:]
    padded = jnp.concatenate([jnp.zeros((conv_size - 1, width_xbc), proj.dtype), conv_in], 0)
    seg_pad = jnp.concatenate([jnp.full((conv_size - 1,), -1, jnp.int32), seg_rows.astype(jnp.int32)], 0)
    conv_pre = conv_bias + conv_weight[conv_size - 1] * conv_in
    for offset in range(1, conv_size):
        begin = conv_size - 1 - offset
        earlier = padded[begin:begin + tok_count]
        same_seg = (seg_pad[begin:begin + tok_count] == seg_rows).astype(proj.dtype)
        conv_pre = conv_pre + conv_weight[conv_size - 1 - offset] * earlier * same_seg[:, None]
    conv_out = jax.nn.silu(conv_pre)
    head_flat = conv_out[:, :inner_size]
    input_map = conv_out[:, inner_size:inner_size + state_size]
    output_map = conv_out[:, inner_size + state_size:]
    step_size = jax.nn.softplus(step_raw + step_bias)
    log_rate = -step_size * jnp.exp(decay_log)
    scan_out = span_scan(head_flat, step_size, log_rate, input_map, output_map, seg_rows, span_len, head_count)
    skip_wide = jnp.repeat(skip_gain, head_size)
    scan_out = scan_out + skip_wide[None, :] * head_flat
    gated = scan_out * jax.nn.silu(gate_in)
    return gated * lax.rsqrt(lax.optimization_barrier(jnp.mean(gated * gated, -1, keepdims=True)) + epsilon) * gate_gain

def layer(hidden_in, in_weight, out_weight, conv_weight, conv_bias, norm_gain, gate_gain, step_bias, decay_log, skip_gain, seg_rows):
    highest = lax.Precision.HIGHEST
    normed = low(hidden_in * lax.rsqrt(lax.optimization_barrier(jnp.mean(hidden_in * hidden_in, -1, keepdims=True)) + epsilon) * norm_gain)
    proj = low_back(jnp.dot(normed, in_weight, precision=highest, preferred_element_type=jnp.float32))
    gated_out = low(mixer(proj, conv_weight, conv_bias, step_bias, decay_log, skip_gain, gate_gain, seg_rows, SPAN))
    branch = low_back(jnp.dot(gated_out, out_weight, precision=highest, preferred_element_type=jnp.float32))
    return hidden_in + branch

def reference(tokens, segment_ids, in_weight, out_weight, conv_weight, conv_bias, norm_gain, gate_gain, step_bias, decay_log, skip_gain, cotangent):
    weights = tuple((value.astype(jnp.float32) for value in (in_weight, out_weight, conv_weight, conv_bias, norm_gain, gate_gain))) + (step_bias, decay_log, skip_gain)
    block_count = TOKENS // TOK_DEV
    hidden_blocks = tokens.astype(jnp.float32).reshape(block_count, TOK_DEV, D)
    seg_blocks = segment_ids.astype(jnp.int32).reshape(block_count, TOK_DEV)
    cot_blocks = cotangent.astype(jnp.float32).reshape(block_count, TOK_DEV, D)

    def one_block(totals, block_item):
        hidden_in, seg_rows, cot_rows = block_item

        def forward(hidden_rows, *params):
            return layer(hidden_rows, *params, seg_rows)
        result, pullback = jax.vjp(forward, hidden_in, *weights)
        grads = pullback(cot_rows)
        totals = tuple((total + grad for total, grad in zip(totals, grads[1:])))
        return (totals, (result, grads[0]))
    start_totals = tuple((jnp.zeros(value.shape, jnp.float32) for value in weights))
    totals, (results, input_grads) = lax.scan(one_block, start_totals, (hidden_blocks, seg_blocks, cot_blocks))
    mixed = results.reshape(TOKENS, D).astype(jnp.bfloat16)
    grad_tokens = input_grads.reshape(TOKENS, D).astype(jnp.bfloat16)
    return (mixed, grad_tokens, totals[0], totals[1], totals[2], totals[3], totals[4], totals[5], totals[6], totals[7], totals[8])
```

```python
import functools

import jax
import jax.numpy as jnp
from jax import lax
from jax.experimental import pallas as pl
from jax.experimental.pallas import tpu as pltpu
from jax.sharding import PartitionSpec as P

CHUNK = 128
F32 = jnp.float32
BF16 = jnp.bfloat16
epsilon = 1e-05


def dot_at(a, b, a_dim, b_dim):
    return lax.dot_general(
        a.astype(BF16), b.astype(BF16), (((a_dim,), (b_dim,)), ((), ())), preferred_element_type=F32
    )


def two_part(values, table, table_dim):
    high = values.astype(BF16)
    low = (values - high.astype(F32)).astype(BF16)
    return dot_at(high, table, 1, table_dim) + dot_at(low, table, 1, table_dim)


def chunk_mask(seg_col, seg_row):
    size = seg_col.shape[0]
    rows = lax.broadcasted_iota(jnp.int32, (size, size), 0)
    cols = lax.broadcasted_iota(jnp.int32, (size, size), 1)
    return (seg_col == seg_row) & (rows >= cols)


def scan_kernel(
    u_ref, b_ref, c_ref, cum_ref, cumt_ref, din_ref, dout_ref, keep_ref, segc_ref, segr_ref, table_ref,
    y_ref, held_ref, state_ref,
):
    @pl.when(pl.program_id(0) == 0)
    def _():
        state_ref[...] = jnp.zeros_like(state_ref)

    table = table_ref[...]
    b_part, c_part = b_ref[...], c_ref[...]
    mask = chunk_mask(segc_ref[...], segr_ref[...])
    scores = jnp.where(mask, dot_at(c_part, b_part, 1, 1), 0.0)
    state = state_ref[...]
    state_low = state.astype(BF16)
    held_ref[0] = state_low
    y_ref[...] = dot_at(c_part, state_low, 1, 0) * two_part(din_ref[...], table, 0)
    cum, cumt = cum_ref[...], cumt_ref[...]
    size = cum.shape[0]
    heads = cum.shape[1]
    first = lax.broadcasted_iota(jnp.int32, (size, 128), 1) < 64
    for pair in range(heads // 2):
        lanes = slice(pair * 128, pair * 128 + 128)
        u_low = u_ref[:, lanes].astype(BF16)
        parts = []
        for head in (2 * pair, 2 * pair + 1):
            gap = cum[:, head : head + 1] - cumt[head : head + 1, :]
            parts.append(dot_at(scores * jnp.exp(jnp.minimum(gap, 0.0)), u_low, 1, 0))
        y_ref[:, lanes] += jnp.where(first, parts[0], parts[1])
    keep_wide = two_part(keep_ref[0], table, 0)[:1]
    weighted = u_ref[...] * two_part(dout_ref[...], table, 0)
    state_ref[...] = state * keep_wide + dot_at(b_part, weighted, 0, 0)


def scan_back_kernel(
    u_ref, b_ref, c_ref, cum_ref, cumt_ref, din_ref, dout_ref, keep_ref, segc_ref, segr_ref, table_ref,
    held_ref, dy_ref,
    du_ref, db_ref, dc_ref, drow_ref, dcol_ref, ddin_ref, ddout_ref, dkeep_ref, dstate_ref,
):
    @pl.when(pl.program_id(0) == 0)
    def _():
        dstate_ref[...] = jnp.zeros_like(dstate_ref)

    table = table_ref[...]
    b_part, c_part = b_ref[...].astype(BF16), c_ref[...].astype(BF16)
    mask = chunk_mask(segc_ref[...], segr_ref[...])
    scores = jnp.where(mask, dot_at(c_part, b_part, 1, 1), 0.0)
    state_low = held_ref[0]
    dstate = dstate_ref[...]
    dstate_low = dstate.astype(BF16)
    u_all, dy_all = u_ref[...], dy_ref[...]
    in_wide = two_part(din_ref[...], table, 0)
    out_wide = two_part(dout_ref[...], table, 0)
    keep_wide = two_part(keep_ref[0], table, 0)[:1]
    carried = dot_at(c_part, state_low, 1, 0)
    ddin_ref[...] = two_part(dy_all * carried, table, 1)
    sent = dot_at(b_part, dstate_low, 1, 0)
    ddout_ref[...] = two_part(u_all * sent, table, 1)
    du_ref[...] = sent * out_wide
    dkeep = jnp.sum(dstate * state_low.astype(F32), axis=0, keepdims=True)
    dkeep_ref[0] = two_part(jnp.broadcast_to(dkeep, (8, dkeep.shape[1])), table, 1)
    dy_in = (dy_all * in_wide).astype(BF16)
    u_out = (u_all * out_wide).astype(BF16)
    dc_carry = dot_at(dy_in, state_low, 1, 1)
    db_carry = dot_at(u_out, dstate_low, 1, 1)
    dstate_ref[...] = dstate * keep_wide + dot_at(c_part, dy_in, 0, 0)
    cum, cumt = cum_ref[...], cumt_ref[...]
    size = cum.shape[0]
    heads = cum.shape[1]
    first = lax.broadcasted_iota(jnp.int32, (size, 128), 1) < 64
    dscores = jnp.zeros((size, size), F32)
    for pair in range(heads // 2):
        lanes = slice(pair * 128, pair * 128 + 128)
        u_low = u_ref[:, lanes].astype(BF16)
        dy_pair = dy_ref[:, lanes]
        dy_low = dy_pair.astype(BF16)
        parts = []
        for side, head in enumerate((2 * pair, 2 * pair + 1)):
            gap = cum[:, head : head + 1] - cumt[head : head + 1, :]
            decay = jnp.exp(jnp.minimum(gap, 0.0))
            mixing = scores * decay
            parts.append(dot_at(mixing, dy_low, 0, 0))
            own = jnp.where(first if side == 0 else jnp.logical_not(first), dy_pair, 0.0)
            dmix = dot_at(own, u_low, 1, 1)
            dscores = dscores + dmix * decay
            weights = dmix * mixing
            drow_ref[:, head : head + 1] = jnp.sum(weights, axis=1, keepdims=True)
            dcol_ref[head : head + 1, :] = jnp.sum(weights, axis=0, keepdims=True)
        du_ref[:, lanes] += jnp.where(first, parts[0], parts[1])
    dscores = jnp.where(mask, dscores, 0.0)
    dc_ref[...] = dc_carry + dot_at(dscores, b_part, 1, 0)
    db_ref[...] = db_carry + dot_at(dscores, c_part, 0, 0)


def scan_specs(count, inner, heads, states, order):
    return [
        pl.BlockSpec((CHUNK, inner), lambda i: (order(i), 0)),
        pl.BlockSpec((CHUNK, states), lambda i: (order(i), 0)),
        pl.BlockSpec((CHUNK, states), lambda i: (order(i), 0)),
        pl.BlockSpec((CHUNK, heads), lambda i: (order(i), 0)),
        pl.BlockSpec((heads, CHUNK), lambda i: (0, order(i))),
        pl.BlockSpec((CHUNK, heads), lambda i: (order(i), 0)),
        pl.BlockSpec((CHUNK, heads), lambda i: (order(i), 0)),
        pl.BlockSpec((1, 8, heads), lambda i: (order(i), 0, 0)),
        pl.BlockSpec((CHUNK, 1), lambda i: (order(i), 0)),
        pl.BlockSpec((1, CHUNK), lambda i: (0, order(i))),
        pl.BlockSpec((heads, inner), lambda i: (0, 0)),
    ]


def scan_forward(pieces):
    u = pieces[0]
    toks, inner = u.shape
    states, heads = pieces[1].shape[1], pieces[3].shape[1]
    count = toks // CHUNK
    return pl.pallas_call(
        scan_kernel,
        grid=(count,),
        in_specs=scan_specs(count, inner, heads, states, lambda i: i),
        out_specs=[
            pl.BlockSpec((CHUNK, inner), lambda i: (i, 0)),
            pl.BlockSpec((1, states, inner), lambda i: (i, 0, 0)),
        ],
        out_shape=[
            jax.ShapeDtypeStruct((toks, inner), F32),
            jax.ShapeDtypeStruct((count, states, inner), BF16),
        ],
        scratch_shapes=[pltpu.VMEM((states, inner), F32)],
        compiler_params=pltpu.CompilerParams(vmem_limit_bytes=48 * 2**20),
        cost_estimate=pl.CostEstimate(flops=6 * 10**9, bytes_accessed=24 * 10**6, transcendentals=4 * 10**6),
    )(*pieces)


def scan_backward(pieces, held, dy):
    u = pieces[0]
    toks, inner = u.shape
    states, heads = pieces[1].shape[1], pieces[3].shape[1]
    count = toks // CHUNK
    order = lambda i: count - 1 - i
    wide = pl.BlockSpec((CHUNK, inner), lambda i: (order(i), 0))
    state_cols = pl.BlockSpec((CHUNK, states), lambda i: (order(i), 0))
    head_cols = pl.BlockSpec((CHUNK, heads), lambda i: (order(i), 0))
    return pl.pallas_call(
        scan_back_kernel,
        grid=(count,),
        in_specs=scan_specs(count, inner, heads, states, order)
        + [pl.BlockSpec((1, states, inner), lambda i: (order(i), 0, 0)), wide],
        out_specs=[
            wide,
            state_cols,
            state_cols,
            head_cols,
            pl.BlockSpec((heads, CHUNK), lambda i: (0, order(i))),
            head_cols,
            head_cols,
            pl.BlockSpec((1, 8, heads), lambda i: (order(i), 0, 0)),
        ],
        out_shape=[
            jax.ShapeDtypeStruct((toks, inner), F32),
            jax.ShapeDtypeStruct((toks, states), F32),
            jax.ShapeDtypeStruct((toks, states), F32),
            jax.ShapeDtypeStruct((toks, heads), F32),
            jax.ShapeDtypeStruct((heads, toks), F32),
            jax.ShapeDtypeStruct((toks, heads), F32),
            jax.ShapeDtypeStruct((toks, heads), F32),
            jax.ShapeDtypeStruct((count, 8, heads), F32),
        ],
        scratch_shapes=[pltpu.VMEM((states, inner), F32)],
        compiler_params=pltpu.CompilerParams(vmem_limit_bytes=48 * 2**20),
        cost_estimate=pl.CostEstimate(flops=20 * 10**9, bytes_accessed=40 * 10**6, transcendentals=4 * 10**6),
    )(*pieces, held, dy)


def before_scan(conv_in, step_raw, conv_weight, conv_bias, step_bias, decay_log, seg_rows, inner_size):
    width_xbc = conv_weight.shape[1]
    conv_size = conv_weight.shape[0]
    state_size = (width_xbc - inner_size) // 2
    tok_count = conv_in.shape[0]
    head_count = step_bias.shape[0]
    head_size = inner_size // head_count
    count = tok_count // CHUNK
    padded = jnp.concatenate([jnp.zeros((conv_size - 1, width_xbc), F32), conv_in], 0)
    seg_pad = jnp.concatenate([jnp.full((conv_size - 1,), -1, jnp.int32), seg_rows], 0)
    conv_pre = conv_bias + conv_weight[conv_size - 1] * conv_in
    for offset in range(1, conv_size):
        begin = conv_size - 1 - offset
        earlier = padded[begin : begin + tok_count]
        same_seg = (seg_pad[begin : begin + tok_count] == seg_rows).astype(F32)
        conv_pre = conv_pre + conv_weight[begin] * earlier * same_seg[:, None]
    conv_out = jax.nn.silu(conv_pre)
    head_flat = conv_out[:, :inner_size]
    input_map = conv_out[:, inner_size : inner_size + state_size]
    output_map = conv_out[:, inner_size + state_size :]
    step_size = jax.nn.softplus(step_raw + step_bias)
    log_rate = -step_size * jnp.exp(decay_log)
    lower = jnp.tril(jnp.ones((CHUNK, CHUNK), F32))
    cum = jnp.einsum(
        "ts,csh->cth", lower, log_rate.reshape(count, CHUNK, head_count), precision=lax.Precision.HIGHEST
    )
    seg_chunks = seg_rows.reshape(count, CHUNK)
    final = seg_chunks[:, -1]
    prior = jnp.concatenate([jnp.full((1,), -1, jnp.int32), final[:-1]])
    last = cum[:, -1:, :]
    entering = (seg_chunks == prior[:, None]).astype(F32)[:, :, None]
    leaving = (seg_chunks == final[:, None]).astype(F32)[:, :, None]
    d_in = (jnp.exp(cum) * entering).reshape(tok_count, head_count)
    d_out = (jnp.exp(last - cum) * leaving).reshape(tok_count, head_count)
    keep = jnp.exp(last[:, 0, :]) * (final == prior).astype(F32)[:, None]
    scaled = head_flat * jnp.repeat(step_size, head_size, axis=1)
    return scaled, input_map, output_map, cum.reshape(tok_count, head_count), d_in, d_out, keep, head_flat


def after_scan(scan_y, head_flat, gate_in, skip_gain, gate_gain):
    head_size = head_flat.shape[1] // skip_gain.shape[0]
    scan_out = scan_y + jnp.repeat(skip_gain, head_size)[None, :] * head_flat
    gated = scan_out * jax.nn.silu(gate_in)
    return gated * lax.rsqrt(jnp.mean(gated * gated, -1, keepdims=True) + epsilon) * gate_gain


def mixer_forward(gate_in, conv_in, step_raw, conv_w, conv_b, step_bias, decay_log, skip_gain, gate_gain, seg):
    inner = gate_in.shape[1]
    toks = gate_in.shape[0]
    heads = step_bias.shape[0]
    pre = lambda *vals: before_scan(*vals, seg, inner)
    (u, b, c, cum, d_in, d_out, keep, head_flat), pre_back = jax.vjp(
        pre, conv_in, step_raw, conv_w, conv_b, step_bias, decay_log
    )
    table = jnp.repeat(jnp.eye(heads, dtype=BF16), inner // heads, axis=1)
    keep_rows = jnp.broadcast_to(keep[:, None, :], (keep.shape[0], 8, heads))
    pieces = (u, b, c, cum, cum.T, d_in, d_out, keep_rows, seg.reshape(toks, 1), seg.reshape(1, toks), table)
    scan_y, held = scan_forward(pieces)
    gated, post_back = jax.vjp(after_scan, scan_y, head_flat, gate_in, skip_gain, gate_gain)

    def scan_back(dy, dhead):
        du, db, dc, drow, dcol, ddin, ddout, dkeep = scan_backward(pieces, held, dy)
        return pre_back((du, db, dc, drow - dcol.T, ddin, ddout, dkeep[:, 0, :], dhead))

    return gated, post_back, scan_back


def rms_rows(values, gain):
    return values * lax.rsqrt(jnp.mean(values * values, -1, keepdims=True) + epsilon) * gain


def bit_steps(first_axis):
    fs = lax.axis_size("fsdp").bit_length() - 1
    rp = lax.axis_size("rep").bit_length() - 1
    reps = [("rep", bit) for bit in reversed(range(rp))]
    rest = [("fsdp", bit) for bit in range(1, fs)]
    if first_axis == "rep":
        return [("fsdp", 0)] + reps + rest
    return [("fsdp", 0)] + rest[:1] + reps + rest[1:]


def partner_list(axis, bit):
    return [(i, i ^ (1 << bit)) for i in range(lax.axis_size(axis))]


def halving_sum(values, first_axis):
    sizes = {"fsdp": lax.axis_size("fsdp").bit_length() - 1, "rep": lax.axis_size("rep").bit_length() - 1}
    dims = [("fsdp", bit) for bit in reversed(range(sizes["fsdp"]))]
    dims += [("rep", bit) for bit in reversed(range(sizes["rep"]))]
    rows = values.shape[0] >> len(dims)
    values = values.reshape((2,) * len(dims) + (rows, values.shape[1]))
    for axis, bit in bit_steps(first_axis):
        at = dims.index((axis, bit))
        mine = (lax.axis_index(axis) >> bit) & 1
        sent = lax.dynamic_index_in_dim(values, 1 - mine, at, keepdims=False).astype(BF16)
        kept = lax.dynamic_index_in_dim(values, mine, at, keepdims=False)
        values = kept + lax.ppermute(sent, axis, partner_list(axis, bit)).astype(F32)
        dims.pop(at)
    return values


def butterfly_sum(values):
    for axis, bit in bit_steps("rep"):
        values = values + lax.ppermute(values, axis, partner_list(axis, bit))
    return values


def local(
    tokens, segment_ids, in_weight, out_weight, conv_weight, conv_bias, norm_gain, gate_gain,
    step_bias, decay_log, skip_gain, cotangent,
):
    axes = ("fsdp", "rep")
    devices = lax.axis_size("fsdp") * lax.axis_size("rep")
    me = lax.axis_index("fsdp") * lax.axis_size("rep") + lax.axis_index("rep")
    rows, width = in_weight.shape
    spare = -width % 128
    smalls = [conv_weight.reshape(-1), conv_bias, norm_gain, gate_gain]
    cuts = [s.shape[0] for s in smalls]
    flat = jnp.concatenate(smalls)
    flat = jnp.pad(flat, (0, rows * spare - flat.shape[0])).reshape(rows, spare)
    in_full = lax.all_gather(jnp.concatenate([in_weight, flat], 1), axes, axis=0, tiled=True)
    out_t = lax.all_gather(out_weight.T, axes, axis=0, tiled=True)
    inner = gate_gain.shape[0] * devices
    taps, chans = conv_weight.shape
    xbc = chans * devices
    flat_all = in_full[:, width:].reshape(devices, rows * spare).astype(F32)
    ends = [sum(cuts[: i + 1]) for i in range(4)]
    conv_full = flat_all[:, : ends[0]].reshape(devices, taps, chans).transpose(1, 0, 2).reshape(taps, xbc)
    bias_full = flat_all[:, ends[0] : ends[1]].reshape(-1)
    norm_full = flat_all[:, ends[1] : ends[2]].reshape(-1)
    gate_full = flat_all[:, ends[2] : ends[3]].reshape(-1)

    hidden_in = tokens.astype(F32)
    normed, norm_pullback = jax.vjp(rms_rows, hidden_in, norm_full)
    normed_low = normed.astype(BF16)
    gate_w, conv_w = in_full[:, :inner], in_full[:, inner:]
    gate_in = jnp.dot(normed_low, gate_w, preferred_element_type=F32)
    rest = jnp.dot(normed_low, conv_w, preferred_element_type=F32)
    gated, post_back, scan_back = mixer_forward(
        gate_in, rest[:, :xbc], rest[:, xbc : width - inner], conv_full, bias_full,
        step_bias, decay_log, skip_gain, gate_full, segment_ids,
    )
    gated_low = gated.astype(BF16)
    grad_gated = jnp.dot(cotangent, out_t, preferred_element_type=F32)
    dy, dhead, dgate, grad_skip, grad_gate = post_back(grad_gated)
    contract_tok = (((0,), (0,)), ((), ()))
    dgate_low = dgate.astype(BF16)
    grad_w_out = lax.dot_general(cotangent, gated_low, contract_tok, preferred_element_type=F32)
    grad_w_gate = lax.dot_general(normed_low, dgate_low, contract_tok, preferred_element_type=F32)
    share_out = halving_sum(grad_w_out, "fsdp")
    share_gate = halving_sum(grad_w_gate, "rep")
    branch = lax.dot_general(gated_low, out_t, (((1,), (1,)), ((), ())), preferred_element_type=F32)
    mixed = (hidden_in + branch).astype(BF16)

    dconv, dstep, grad_conv_w, grad_conv_b, grad_step, grad_decay = scan_back(dy, dhead)
    drest = jnp.concatenate([dconv, dstep], 1).astype(BF16)
    drest = jnp.pad(drest, ((0, 0), (0, spare)))
    half = xbc // 256 * 128
    share_a = halving_sum(
        lax.dot_general(normed_low, drest[:, :half], contract_tok, preferred_element_type=F32), "rep"
    )
    share_b = halving_sum(
        lax.dot_general(normed_low, drest[:, half:], contract_tok, preferred_element_type=F32), "fsdp"
    )
    contract_col = (((1,), (1,)), ((), ()))
    grad_normed = lax.dot_general(dgate_low, gate_w, contract_col, preferred_element_type=F32)
    grad_normed = grad_normed + lax.dot_general(drest, conv_w, contract_col, preferred_element_type=F32)
    grad_hidden, grad_norm = norm_pullback(grad_normed)
    grad_tokens = (cotangent.astype(F32) + grad_hidden).astype(BF16)
    flat_grads = [grad_conv_w.reshape(-1), grad_conv_b, grad_norm, grad_gate, grad_step, grad_decay, grad_skip]
    sizes = [g.shape[0] for g in flat_grads]
    total = butterfly_sum(jnp.concatenate(flat_grads))
    starts = [sum(sizes[:i]) for i in range(len(sizes))]
    sums = [total[s : s + n] for s, n in zip(starts, sizes)]
    mine = lambda vec, n: lax.dynamic_slice_in_dim(vec, me * n, n, vec.ndim - 1)
    share_in = jnp.concatenate([share_gate, share_a, share_b], 1)[:, :width]
    return (
        mixed,
        grad_tokens,
        share_in,
        share_out.T,
        mine(sums[0].reshape(taps, xbc), chans),
        mine(sums[1], chans),
        mine(sums[2], norm_gain.shape[0]),
        mine(sums[3], gate_gain.shape[0]),
        sums[4],
        sums[5],
        sums[6],
    )


def solution(mesh):
    in_specs = (
        P(("fsdp", "rep"), None),
        P(("fsdp", "rep")),
        P(("fsdp", "rep"), None),
        P(None, ("fsdp", "rep")),
        P(None, ("fsdp", "rep")),
        P(("fsdp", "rep")),
        P(("fsdp", "rep")),
        P(("fsdp", "rep")),
        P(),
        P(),
        P(),
        P(("fsdp", "rep"), None),
    )
    out_specs = (
        P(("fsdp", "rep"), None),
        P(("fsdp", "rep"), None),
        P(("fsdp", "rep"), None),
        P(None, ("fsdp", "rep")),
        P(None, ("fsdp", "rep")),
        P(("fsdp", "rep")),
        P(("fsdp", "rep")),
        P(("fsdp", "rep")),
        P(),
        P(),
        P(),
    )
    return jax.shard_map(local, mesh=mesh, in_specs=in_specs, out_specs=out_specs, check_vma=False)
```

```python
import functools

import jax
import jax.numpy as jnp
from jax import lax
from jax.experimental import pallas as pl
from jax.experimental.pallas import tpu as pltpu
from jax.sharding import PartitionSpec as P

CHUNK = 128
F32 = jnp.float32
BF16 = jnp.bfloat16
epsilon = 1e-05


def dot_at(a, b, a_dim, b_dim):
    return lax.dot_general(
        a.astype(BF16), b.astype(BF16), (((a_dim,), (b_dim,)), ((), ())), preferred_element_type=F32
    )


def two_part(values, table, table_dim):
    high = values.astype(BF16)
    low = (values - high.astype(F32)).astype(BF16)
    return dot_at(high, table, 1, table_dim) + dot_at(low, table, 1, table_dim)


def chunk_mask(seg_col, seg_row):
    size = seg_col.shape[0]
    rows = lax.broadcasted_iota(jnp.int32, (size, size), 0)
    cols = lax.broadcasted_iota(jnp.int32, (size, size), 1)
    return (seg_col == seg_row) & (rows >= cols)


def scan_kernel(
    x_ref, b_ref, c_ref, cum_ref, cumt_ref, din_ref, dout_ref, keep_ref, segc_ref, segr_ref, table_ref, dt_ref,
    y_ref, held_ref, state_ref, u_ref,
):
    @pl.when(pl.program_id(0) == 0)
    def _():
        state_ref[...] = jnp.zeros_like(state_ref)

    table = table_ref[...]
    u_ref[...] = x_ref[...] * two_part(dt_ref[...], table, 0)
    b_part, c_part = b_ref[...], c_ref[...]
    mask = chunk_mask(segc_ref[...], segr_ref[...])
    scores = jnp.where(mask, dot_at(c_part, b_part, 1, 1), 0.0)
    state = state_ref[...]
    state_low = state.astype(BF16)
    held_ref[0] = state_low
    y_ref[...] = dot_at(c_part, state_low, 1, 0) * two_part(din_ref[...], table, 0)
    cum, cumt = cum_ref[...], cumt_ref[...]
    size = cum.shape[0]
    heads = cum.shape[1]
    first = lax.broadcasted_iota(jnp.int32, (size, 128), 1) < 64
    for pair in range(heads // 2):
        lanes = slice(pair * 128, pair * 128 + 128)
        u_low = u_ref[:, lanes].astype(BF16)
        parts = []
        for head in (2 * pair, 2 * pair + 1):
            gap = cum[:, head : head + 1] - cumt[head : head + 1, :]
            parts.append(dot_at(scores * jnp.exp(jnp.minimum(gap, 0.0)), u_low, 1, 0))
        y_ref[:, lanes] += jnp.where(first, parts[0], parts[1])
    keep_wide = two_part(keep_ref[0], table, 0)[:1]
    weighted = u_ref[...] * two_part(dout_ref[...], table, 0)
    state_ref[...] = state * keep_wide + dot_at(b_part, weighted, 0, 0)


def scan_back_kernel(
    x_ref, b_ref, c_ref, cum_ref, cumt_ref, din_ref, dout_ref, keep_ref, segc_ref, segr_ref, table_ref, dt_ref,
    held_ref, dy_ref,
    dx_ref, db_ref, dc_ref, drow_ref, dcol_ref, ddin_ref, ddout_ref, dkeep_ref, ddt_ref, dstate_ref, u_ref, du_ref,
):
    @pl.when(pl.program_id(0) == 0)
    def _():
        dstate_ref[...] = jnp.zeros_like(dstate_ref)

    table = table_ref[...]
    dt_wide = two_part(dt_ref[...], table, 0)
    u_ref[...] = x_ref[...] * dt_wide
    b_part, c_part = b_ref[...].astype(BF16), c_ref[...].astype(BF16)
    mask = chunk_mask(segc_ref[...], segr_ref[...])
    scores = jnp.where(mask, dot_at(c_part, b_part, 1, 1), 0.0)
    state_low = held_ref[0]
    dstate = dstate_ref[...]
    dstate_low = dstate.astype(BF16)
    u_all, dy_all = u_ref[...], dy_ref[...]
    in_wide = two_part(din_ref[...], table, 0)
    out_wide = two_part(dout_ref[...], table, 0)
    keep_wide = two_part(keep_ref[0], table, 0)[:1]
    carried = dot_at(c_part, state_low, 1, 0)
    ddin_ref[...] = two_part(dy_all * carried, table, 1)
    sent = dot_at(b_part, dstate_low, 1, 0)
    ddout_ref[...] = two_part(u_all * sent, table, 1)
    du_ref[...] = sent * out_wide
    dkeep = jnp.sum(dstate * state_low.astype(F32), axis=0, keepdims=True)
    dkeep_ref[0] = two_part(jnp.broadcast_to(dkeep, (8, dkeep.shape[1])), table, 1)
    dy_in = (dy_all * in_wide).astype(BF16)
    u_out = (u_all * out_wide).astype(BF16)
    dc_carry = dot_at(dy_in, state_low, 1, 1)
    db_carry = dot_at(u_out, dstate_low, 1, 1)
    dstate_ref[...] = dstate * keep_wide + dot_at(c_part, dy_in, 0, 0)
    cum, cumt = cum_ref[...], cumt_ref[...]
    size = cum.shape[0]
    heads = cum.shape[1]
    first = lax.broadcasted_iota(jnp.int32, (size, 128), 1) < 64
    dscores = jnp.zeros((size, size), F32)
    for pair in range(heads // 2):
        lanes = slice(pair * 128, pair * 128 + 128)
        u_low = u_ref[:, lanes].astype(BF16)
        dy_pair = dy_ref[:, lanes]
        dy_low = dy_pair.astype(BF16)
        parts = []
        for side, head in enumerate((2 * pair, 2 * pair + 1)):
            gap = cum[:, head : head + 1] - cumt[head : head + 1, :]
            decay = jnp.exp(jnp.minimum(gap, 0.0))
            mixing = scores * decay
            parts.append(dot_at(mixing, dy_low, 0, 0))
            own = jnp.where(first if side == 0 else jnp.logical_not(first), dy_pair, 0.0)
            dmix = dot_at(own, u_low, 1, 1)
            dscores = dscores + dmix * decay
            weights = dmix * mixing
            drow_ref[:, head : head + 1] = jnp.sum(weights, axis=1, keepdims=True)
            dcol_ref[head : head + 1, :] = jnp.sum(weights, axis=0, keepdims=True)
        du_ref[:, lanes] += jnp.where(first, parts[0], parts[1])
    dscores = jnp.where(mask, dscores, 0.0)
    dc_ref[...] = dc_carry + dot_at(dscores, b_part, 1, 0)
    db_ref[...] = db_carry + dot_at(dscores, c_part, 0, 0)
    du_all = du_ref[...]
    dx_ref[...] = du_all * dt_wide
    ddt_ref[...] = two_part(du_all * x_ref[...], table, 1)


def scan_specs(count, inner, heads, states, order):
    return [
        pl.BlockSpec((CHUNK, inner), lambda i: (order(i), 0)),
        pl.BlockSpec((CHUNK, states), lambda i: (order(i), 0)),
        pl.BlockSpec((CHUNK, states), lambda i: (order(i), 0)),
        pl.BlockSpec((CHUNK, heads), lambda i: (order(i), 0)),
        pl.BlockSpec((heads, CHUNK), lambda i: (0, order(i))),
        pl.BlockSpec((CHUNK, heads), lambda i: (order(i), 0)),
        pl.BlockSpec((CHUNK, heads), lambda i: (order(i), 0)),
        pl.BlockSpec((1, 8, heads), lambda i: (order(i), 0, 0)),
        pl.BlockSpec((CHUNK, 1), lambda i: (order(i), 0)),
        pl.BlockSpec((1, CHUNK), lambda i: (0, order(i))),
        pl.BlockSpec((heads, inner), lambda i: (0, 0)),
        pl.BlockSpec((CHUNK, heads), lambda i: (order(i), 0)),
    ]


def scan_forward(pieces):
    u = pieces[0]
    toks, inner = u.shape
    states, heads = pieces[1].shape[1], pieces[3].shape[1]
    count = toks // CHUNK
    return pl.pallas_call(
        scan_kernel,
        grid=(count,),
        in_specs=scan_specs(count, inner, heads, states, lambda i: i),
        out_specs=[
            pl.BlockSpec((CHUNK, inner), lambda i: (i, 0)),
            pl.BlockSpec((1, states, inner), lambda i: (i, 0, 0)),
        ],
        out_shape=[
            jax.ShapeDtypeStruct((toks, inner), F32),
            jax.ShapeDtypeStruct((count, states, inner), BF16),
        ],
        scratch_shapes=[pltpu.VMEM((states, inner), F32), pltpu.VMEM((CHUNK, inner), F32)],
        compiler_params=pltpu.CompilerParams(vmem_limit_bytes=48 * 2**20),
        cost_estimate=pl.CostEstimate(flops=6 * 10**9, bytes_accessed=24 * 10**6, transcendentals=4 * 10**6),
    )(*pieces)


def scan_backward(pieces, held, dy):
    u = pieces[0]
    toks, inner = u.shape
    states, heads = pieces[1].shape[1], pieces[3].shape[1]
    count = toks // CHUNK
    order = lambda i: count - 1 - i
    wide = pl.BlockSpec((CHUNK, inner), lambda i: (order(i), 0))
    state_cols = pl.BlockSpec((CHUNK, states), lambda i: (order(i), 0))
    head_cols = pl.BlockSpec((CHUNK, heads), lambda i: (order(i), 0))
    return pl.pallas_call(
        scan_back_kernel,
        grid=(count,),
        in_specs=scan_specs(count, inner, heads, states, order)
        + [pl.BlockSpec((1, states, inner), lambda i: (order(i), 0, 0)), wide],
        out_specs=[
            wide,
            state_cols,
            state_cols,
            head_cols,
            pl.BlockSpec((heads, CHUNK), lambda i: (0, order(i))),
            head_cols,
            head_cols,
            pl.BlockSpec((1, 8, heads), lambda i: (order(i), 0, 0)),
            head_cols,
        ],
        out_shape=[
            jax.ShapeDtypeStruct((toks, inner), F32),
            jax.ShapeDtypeStruct((toks, states), F32),
            jax.ShapeDtypeStruct((toks, states), F32),
            jax.ShapeDtypeStruct((toks, heads), F32),
            jax.ShapeDtypeStruct((heads, toks), F32),
            jax.ShapeDtypeStruct((toks, heads), F32),
            jax.ShapeDtypeStruct((toks, heads), F32),
            jax.ShapeDtypeStruct((count, 8, heads), F32),
            jax.ShapeDtypeStruct((toks, heads), F32),
        ],
        scratch_shapes=[pltpu.VMEM((states, inner), F32), pltpu.VMEM((CHUNK, inner), F32), pltpu.VMEM((CHUNK, inner), F32)],
        compiler_params=pltpu.CompilerParams(vmem_limit_bytes=48 * 2**20),
        cost_estimate=pl.CostEstimate(flops=20 * 10**9, bytes_accessed=40 * 10**6, transcendentals=4 * 10**6),
    )(*pieces, held, dy)


def before_scan(conv_in, step_raw, conv_weight, conv_bias, step_bias, decay_log, seg_rows, inner_size):
    width_xbc = conv_weight.shape[1]
    conv_size = conv_weight.shape[0]
    state_size = (width_xbc - inner_size) // 2
    tok_count = conv_in.shape[0]
    head_count = step_bias.shape[0]
    count = tok_count // CHUNK
    padded = jnp.concatenate([jnp.zeros((conv_size - 1, width_xbc), F32), conv_in], 0)
    seg_pad = jnp.concatenate([jnp.full((conv_size - 1,), -1, jnp.int32), seg_rows], 0)
    conv_pre = conv_bias + conv_weight[conv_size - 1] * conv_in
    for offset in range(1, conv_size):
        begin = conv_size - 1 - offset
        earlier = padded[begin : begin + tok_count]
        same_seg = (seg_pad[begin : begin + tok_count] == seg_rows).astype(F32)
        conv_pre = conv_pre + conv_weight[begin] * earlier * same_seg[:, None]
    conv_out = jax.nn.silu(conv_pre)
    head_flat = conv_out[:, :inner_size]
    input_map = conv_out[:, inner_size : inner_size + state_size]
    output_map = conv_out[:, inner_size + state_size :]
    step_size = jax.nn.softplus(step_raw + step_bias)
    log_rate = -step_size * jnp.exp(decay_log)
    lower = jnp.tril(jnp.ones((CHUNK, CHUNK), F32))
    cum = jnp.einsum(
        "ts,csh->cth", lower, log_rate.reshape(count, CHUNK, head_count), precision=lax.Precision.HIGHEST
    )
    seg_chunks = seg_rows.reshape(count, CHUNK)
    final = seg_chunks[:, -1]
    prior = jnp.concatenate([jnp.full((1,), -1, jnp.int32), final[:-1]])
    last = cum[:, -1:, :]
    entering = (seg_chunks == prior[:, None]).astype(F32)[:, :, None]
    leaving = (seg_chunks == final[:, None]).astype(F32)[:, :, None]
    d_in = (jnp.exp(cum) * entering).reshape(tok_count, head_count)
    d_out = (jnp.exp(last - cum) * leaving).reshape(tok_count, head_count)
    keep = jnp.exp(last[:, 0, :]) * (final == prior).astype(F32)[:, None]
    return head_flat, input_map, output_map, cum.reshape(tok_count, head_count), d_in, d_out, keep, step_size


def after_scan(scan_y, head_flat, gate_in, skip_gain, gate_gain):
    head_size = head_flat.shape[1] // skip_gain.shape[0]
    scan_out = scan_y + jnp.repeat(skip_gain, head_size)[None, :] * head_flat
    gated = scan_out * jax.nn.silu(gate_in)
    return gated * lax.rsqrt(jnp.mean(gated * gated, -1, keepdims=True) + epsilon) * gate_gain


def mixer_forward(gate_in, conv_in, step_raw, conv_w, conv_b, step_bias, decay_log, skip_gain, gate_gain, seg):
    inner = gate_in.shape[1]
    toks = gate_in.shape[0]
    heads = step_bias.shape[0]
    pre = lambda *vals: before_scan(*vals, seg, inner)
    (head_flat, b, c, cum, d_in, d_out, keep, step_size), pre_back = jax.vjp(
        pre, conv_in, step_raw, conv_w, conv_b, step_bias, decay_log
    )
    table = jnp.repeat(jnp.eye(heads, dtype=BF16), inner // heads, axis=1)
    keep_rows = jnp.broadcast_to(keep[:, None, :], (keep.shape[0], 8, heads))
    pieces = (
        head_flat, b, c, cum, cum.T, d_in, d_out, keep_rows,
        seg.reshape(toks, 1), seg.reshape(1, toks), table, step_size,
    )
    scan_y, held = scan_forward(pieces)
    gated, post_back = jax.vjp(after_scan, scan_y, head_flat, gate_in, skip_gain, gate_gain)

    def scan_back(dy):
        return scan_backward(pieces, held, dy)

    def before_back(grads, dhead):
        dx, db, dc, drow, dcol, ddin, ddout, dkeep, ddt = grads
        return pre_back((dx + dhead, db, dc, drow - dcol.T, ddin, ddout, dkeep[:, 0, :], ddt))

    return gated, post_back, scan_back, before_back


def rms_rows(values, gain):
    return values * lax.rsqrt(jnp.mean(values * values, -1, keepdims=True) + epsilon) * gain


def bit_steps(first_axis):
    fs = lax.axis_size("fsdp").bit_length() - 1
    rp = lax.axis_size("rep").bit_length() - 1
    reps = [("rep", bit) for bit in reversed(range(rp))]
    rest = [("fsdp", bit) for bit in range(1, fs)]
    if first_axis == "rep":
        return [("fsdp", 0)] + reps + rest
    return [("fsdp", 0)] + rest[:1] + reps + rest[1:]


def partner_list(axis, bit):
    return [(i, i ^ (1 << bit)) for i in range(lax.axis_size(axis))]


class HalvingSum:
    def __init__(self, values, first_axis):
        fs = lax.axis_size("fsdp").bit_length() - 1
        rp = lax.axis_size("rep").bit_length() - 1
        self.dims = [("fsdp", bit) for bit in reversed(range(fs))] + [("rep", bit) for bit in reversed(range(rp))]
        rows = values.shape[0] >> len(self.dims)
        self.values = values.reshape((2,) * len(self.dims) + (rows, values.shape[1]))
        self.steps = bit_steps(first_axis)

    def step(self, *beside):
        axis, bit = self.steps.pop(0)
        at = self.dims.index((axis, bit))
        mine = (lax.axis_index(axis) >> bit) & 1
        sent = lax.dynamic_index_in_dim(self.values, 1 - mine, at, keepdims=False).astype(BF16)
        kept = lax.dynamic_index_in_dim(self.values, mine, at, keepdims=False)
        got = lax.ppermute(sent, axis, partner_list(axis, bit))
        if beside:
            got, *beside = lax.optimization_barrier((got, *beside))
        self.values = kept + got.astype(F32)
        self.dims.pop(at)
        return beside

    def finish(self):
        while self.steps:
            self.step()
        return self.values


def butterfly_sum(values):
    for axis, bit in bit_steps("rep"):
        values = values + lax.ppermute(values, axis, partner_list(axis, bit))
    return values


def local(
    tokens, segment_ids, in_weight, out_weight, conv_weight, conv_bias, norm_gain, gate_gain,
    step_bias, decay_log, skip_gain, cotangent,
):
    axes = ("fsdp", "rep")
    devices = lax.axis_size("fsdp") * lax.axis_size("rep")
    me = lax.axis_index("fsdp") * lax.axis_size("rep") + lax.axis_index("rep")
    rows, width = in_weight.shape
    spare = -width % 128
    smalls = [conv_weight.reshape(-1), conv_bias, norm_gain, gate_gain]
    cuts = [s.shape[0] for s in smalls]
    flat = jnp.concatenate(smalls)
    flat = jnp.pad(flat, (0, rows * spare - flat.shape[0])).reshape(rows, spare)
    in_full = lax.all_gather(jnp.concatenate([in_weight, flat], 1), axes, axis=0, tiled=True)
    out_t = lax.all_gather(out_weight.T, axes, axis=0, tiled=True)
    inner = gate_gain.shape[0] * devices
    taps, chans = conv_weight.shape
    xbc = chans * devices
    flat_all = in_full[:, width:].reshape(devices, rows * spare).astype(F32)
    ends = [sum(cuts[: i + 1]) for i in range(4)]
    conv_full = flat_all[:, : ends[0]].reshape(devices, taps, chans).transpose(1, 0, 2).reshape(taps, xbc)
    bias_full = flat_all[:, ends[0] : ends[1]].reshape(-1)
    norm_full = flat_all[:, ends[1] : ends[2]].reshape(-1)
    gate_full = flat_all[:, ends[2] : ends[3]].reshape(-1)

    hidden_in = tokens.astype(F32)
    normed, norm_pullback = jax.vjp(rms_rows, hidden_in, norm_full)
    normed_low = normed.astype(BF16)
    gate_w, conv_w = in_full[:, :inner], in_full[:, inner:]
    gate_in = jnp.dot(normed_low, gate_w, preferred_element_type=F32)
    rest = jnp.dot(normed_low, conv_w, preferred_element_type=F32)
    gated, post_back, scan_back, before_back = mixer_forward(
        gate_in, rest[:, :xbc], rest[:, xbc : width - inner], conv_full, bias_full,
        step_bias, decay_log, skip_gain, gate_full, segment_ids,
    )
    gated_low = gated.astype(BF16)
    grad_gated = jnp.dot(cotangent, out_t, preferred_element_type=F32)
    contract_tok = (((0,), (0,)), ((), ()))
    contract_col = (((1,), (1,)), ((), ()))
    grad_w_out = lax.dot_general(cotangent, gated_low, contract_tok, preferred_element_type=F32)
    sum_out = HalvingSum(grad_w_out, "fsdp")
    dy, dhead, dgate, grad_skip, grad_gate = post_back(grad_gated)
    dgate_low = dgate.astype(BF16)
    dy, dhead, dgate_low = sum_out.step(dy, dhead, dgate_low)
    grad_w_gate = lax.dot_general(normed_low, dgate_low, contract_tok, preferred_element_type=F32)
    sum_gate = HalvingSum(grad_w_gate, "rep")
    branch = lax.dot_general(gated_low, out_t, contract_col, preferred_element_type=F32)
    mixed = (hidden_in + branch).astype(BF16)

    scan_grads = scan_back(dy)
    scan_grads = sum_out.step(*scan_grads)
    scan_grads = sum_gate.step(*scan_grads)
    dconv, dstep, grad_conv_w, grad_conv_b, grad_step, grad_decay = before_back(scan_grads, dhead)
    drest = jnp.concatenate([dconv, dstep], 1).astype(BF16)
    drest = jnp.pad(drest, ((0, 0), (0, spare)))
    (drest,) = sum_out.step(drest)
    (drest,) = sum_gate.step(drest)
    half = xbc // 256 * 128
    grad_a = lax.dot_general(normed_low, drest[:, :half], contract_tok, preferred_element_type=F32)
    grad_b = lax.dot_general(normed_low, drest[:, half:], contract_tok, preferred_element_type=F32)
    grad_a, grad_b = sum_out.step(grad_a, grad_b)
    grad_a, grad_b = sum_gate.step(grad_a, grad_b)
    sum_a, sum_b = HalvingSum(grad_a, "rep"), HalvingSum(grad_b, "fsdp")
    grad_normed = lax.dot_general(dgate_low, gate_w, contract_col, preferred_element_type=F32)
    grad_normed = grad_normed + lax.dot_general(drest, conv_w, contract_col, preferred_element_type=F32)
    for share in (sum_out, sum_gate, sum_a, sum_b):
        (grad_normed,) = share.step(grad_normed)
    grad_hidden, grad_norm = norm_pullback(grad_normed)
    grad_tokens = (cotangent.astype(F32) + grad_hidden).astype(BF16)
    share_out, share_gate = sum_out.finish(), sum_gate.finish()
    share_a, share_b = sum_a.finish(), sum_b.finish()
    flat_grads = [grad_conv_w.reshape(-1), grad_conv_b, grad_norm, grad_gate, grad_step, grad_decay, grad_skip]
    sizes = [g.shape[0] for g in flat_grads]
    total = butterfly_sum(jnp.concatenate(flat_grads))
    starts = [sum(sizes[:i]) for i in range(len(sizes))]
    sums = [total[s : s + n] for s, n in zip(starts, sizes)]
    mine = lambda vec, n: lax.dynamic_slice_in_dim(vec, me * n, n, vec.ndim - 1)
    share_in = jnp.concatenate([share_gate, share_a, share_b], 1)[:, :width]
    return (
        mixed,
        grad_tokens,
        share_in,
        share_out.T,
        mine(sums[0].reshape(taps, xbc), chans),
        mine(sums[1], chans),
        mine(sums[2], norm_gain.shape[0]),
        mine(sums[3], gate_gain.shape[0]),
        sums[4],
        sums[5],
        sums[6],
    )


def solution(mesh):
    in_specs = (
        P(("fsdp", "rep"), None),
        P(("fsdp", "rep")),
        P(("fsdp", "rep"), None),
        P(None, ("fsdp", "rep")),
        P(None, ("fsdp", "rep")),
        P(("fsdp", "rep")),
        P(("fsdp", "rep")),
        P(("fsdp", "rep")),
        P(),
        P(),
        P(),
        P(("fsdp", "rep"), None),
    )
    out_specs = (
        P(("fsdp", "rep"), None),
        P(("fsdp", "rep"), None),
        P(("fsdp", "rep"), None),
        P(None, ("fsdp", "rep")),
        P(None, ("fsdp", "rep")),
        P(("fsdp", "rep")),
        P(("fsdp", "rep")),
        P(("fsdp", "rep")),
        P(),
        P(),
        P(),
    )
    return jax.shard_map(local, mesh=mesh, in_specs=in_specs, out_specs=out_specs, check_vma=False)
```
